512 devices in a mesh: lat: 16 (over z_lo, y), lon: 32 (over x, z_hi, core).
Axes of the slice: x: 4, y: 8, z: 8 (z_hi: 4, z_lo: 2; z = z_hi * 2 + z_lo), core: 2. Of those that a mesh axis runs over, the one named last changes fastest.
Arguments:
- fine_in: bfloat16 [4, 192, 384, 512], P(None, 'lat', 'lon'), may hold values from -6 to 6
- norm_gain: float32 [512], replicated, may hold values from 0.5 to 1.5
- qkv_weight: bfloat16 [512, 1536], replicated, as said below
- proj_weight: bfloat16 [512, 512], replicated, may hold values from -0.25 to 0.25
- merge_gain: float32 [2048], replicated, may hold values from 0.5 to 1.5
- merge_weight: bfloat16 [2048, 1024], P('lon'), may hold values from -0.125 to 0.125
Outputs:
- fine_out: bfloat16 [4, 192, 384, 512], P(None, 'lat', 'lon')
- coarse: bfloat16 [4, 96, 192, 1024], P(None, 'lat', 'lon')
The draws below stay inside these ranges and needn't reach their ends.
Inputs may be any that keep to these rules, and one draw needn't show every extreme that they name: `qkv_weight`: query, key and value projections.
All inputs are finite; a program needn't handle non-finite values.
Results may differ from the reference program's by a relative error of at most 0.0067.
Values may be sent and summed in bfloat16 or wider, within the bound.
A program may use at most 128 MiB of HBM per device.

```python
import jax
import jax.numpy as jnp
from jax import lax

D = 512
HEADS = 8
LEV = 4
NLAT = 192
NLON = 384


def draw_qkv_weight(key, part):
    key = jax.random.fold_in(key, 7)
    first, second, third = jax.random.split(key, 3)
    base = D ** (-0.5)
    query = jax.random.normal(first, (D, D), jnp.float32) * base
    keys = jax.random.normal(second, (D, D), jnp.float32) * base
    values = jax.random.normal(third, (D, D), jnp.float32) * base
    return jnp.concatenate([query, keys, values], 1).astype(jnp.bfloat16)


def block_levels(own_key, extent, shards, low, top_value):
    def one(dim, blocks):
        draws = jax.random.uniform(jax.random.fold_in(jax.random.fold_in(own_key, 6), dim), (blocks,), jnp.float32, low / len(shards), top_value / len(shards))
        return jnp.repeat(jnp.exp(draws), extent[dim] // blocks).reshape((-1,) + (1,) * (len(extent) - dim - 1))

    factor_of = one(*shards[0])
    for cut in shards[1:]:
        factor_of = factor_of * one(*cut)
    return factor_of


def normal_values(stream_key, dims, scale, most, cuts=(), kind=jnp.bfloat16):
    array = scale * jax.random.normal(stream_key, dims, jnp.float32)
    if cuts:
        array = array * block_levels(stream_key, dims, cuts, -0.22, 0.18)
    return jnp.clip(array, -most, most).astype(kind)


def setup_inputs(seed: int = 0) -> dict:
    streams_of = jax.random.split(jax.random.key(seed), 7)
    return {
        "fine_in": normal_values(streams_of[0], (LEV, NLAT, NLON, D), 1.0, 6.0, ((1, 16), (2, 32))),
        "norm_gain": jnp.clip(1.0 + 0.1 * jax.random.normal(streams_of[1], (D,), jnp.float32), 0.5, 1.5),
        "qkv_weight": draw_qkv_weight(jax.random.fold_in(streams_of[6], 71), 0),
        "proj_weight": normal_values(streams_of[3], (D, D), D ** -0.5, 0.25),
        "merge_gain": jnp.clip(1.0 + 0.1 * jax.random.normal(streams_of[4], (4 * D,), jnp.float32), 0.5, 1.5),
        "merge_weight": normal_values(streams_of[5], (4 * D, 2 * D), (4 * D) ** -0.5, 0.125, ((0, 32),)),
    }


def layer_norm(values, gain):
    values = values.astype(jnp.float32)
    mean = lax.optimization_barrier(jnp.mean(values, -1, keepdims=True))
    centered = values - mean
    spread = lax.optimization_barrier(jnp.mean(centered * centered, -1, keepdims=True))
    return centered * lax.rsqrt(spread + 1e-05) * gain

def cell_labels(row_pos, lev, nrows):
    lev_pos = jnp.arange(lev, dtype=jnp.int32)
    lev_label = jnp.where(lev_pos < 2, 0, jnp.where(lev_pos < 3, 1, 2))
    row_label = jnp.where(row_pos < nrows - 12, 0, jnp.where(row_pos < nrows - 6, 1, 2))
    return (lev_label[:, None] * 3 + row_label[None, :]).astype(jnp.int32)

def attend(block, labels, qkv_weight, proj_weight, heads):
    lev, rows, cols, width = block.shape
    size = width // heads
    grid = block.reshape(lev // 2, 2, rows // 12, 12, cols // 6, 6, width)
    grid = grid.transpose(0, 2, 4, 1, 3, 5, 6)
    count = lev // 2 * (rows // 12) * (cols // 6)
    tokens = grid.reshape(count * 144, width)
    marks = labels.reshape(lev // 2, 2, rows // 12, 12).transpose(0, 2, 1, 3)
    marks = jnp.broadcast_to(marks[:, :, None, :, :, None], (lev // 2, rows // 12, cols // 6, 2, 12, 6))
    marks = marks.reshape(count, 144)
    qkv = jnp.dot(tokens, qkv_weight, preferred_element_type=jnp.float32).astype(jnp.bfloat16)
    qkv = qkv.reshape(count, 144, 3, heads, size)
    query = qkv[:, :, 0].astype(jnp.float32)
    keys = qkv[:, :, 1].astype(jnp.float32)
    values = qkv[:, :, 2].astype(jnp.float32)
    scores = jnp.einsum('wqhs,wkhs->whqk', query, keys) * size ** (-0.5)
    same = marks[:, None, :, None] == marks[:, None, None, :]
    scores = jnp.where(same, scores, -1e+30)
    top = lax.optimization_barrier(jnp.max(scores, -1, keepdims=True))
    expo = jnp.exp(scores - top)
    probs = (expo / lax.optimization_barrier(jnp.sum(expo, -1, keepdims=True))).astype(jnp.bfloat16)
    attended = jnp.einsum('whqk,wkhs->wqhs', probs.astype(jnp.float32), values).astype(jnp.bfloat16)
    attended = attended.reshape(count * 144, width)
    branch = jnp.dot(attended, proj_weight, preferred_element_type=jnp.float32).astype(jnp.bfloat16)
    branch = branch.reshape(lev // 2, rows // 12, cols // 6, 2, 12, 6, width)
    return branch.transpose(0, 3, 1, 4, 2, 5, 6).reshape(lev, rows, cols, width)

def reference(fine_in, norm_gain, qkv_weight, proj_weight, merge_gain, merge_weight):
    normed = layer_norm(fine_in, norm_gain).astype(jnp.bfloat16)
    rolled = jnp.roll(normed, (-1, -6, -3), axis=(0, 1, 2))

    def strip(index):
        block = lax.dynamic_slice_in_dim(rolled, index * 12, 12, 1)
        row_pos = (index * 12 + jnp.arange(12, dtype=jnp.int32)).astype(jnp.int32)
        labels = cell_labels(row_pos, LEV, NLAT)
        return attend(block, labels, qkv_weight, proj_weight, HEADS)
    strips = lax.map(strip, jnp.arange(NLAT // 12, dtype=jnp.int32))
    branch = strips.transpose(1, 0, 2, 3, 4).reshape(LEV, NLAT, NLON, D)
    branch = jnp.roll(branch, (1, 6, 3), axis=(0, 1, 2))
    fine_out = (fine_in.astype(jnp.float32) + branch.astype(jnp.float32)).astype(jnp.bfloat16)
    quads = jnp.concatenate([fine_out[:, 0::2, 0::2], fine_out[:, 1::2, 0::2], fine_out[:, 0::2, 1::2], fine_out[:, 1::2, 1::2]], -1)
    mnormed = layer_norm(quads, merge_gain).astype(jnp.bfloat16)
    flat = mnormed.reshape(-1, 4 * D)
    coarse = jnp.dot(flat, merge_weight, preferred_element_type=jnp.float32).astype(jnp.bfloat16)
    return (fine_out, coarse.reshape(LEV, NLAT // 2, NLON // 2, 2 * D))
```

```python
import functools

import jax
import jax.numpy as jnp
import numpy as np
from jax import lax
from jax.experimental import pallas as pl
from jax.experimental.pallas import tpu as pltpu
from jax.sharding import PartitionSpec as P

MESH = pl.DeviceIdType.MESH
BF16 = jnp.bfloat16
F32 = jnp.float32

WIDTH = 512
PAIRS = 4
WIN = 144
LEVELS = ((1, 2), (3, 0))
SLAB = 16
NAT = 2 * 12 * SLAB
S0, L0, D0, K0, C0, PIECES = 0, 112, 160, 208, 288, 336
SENT = ((S0, 112), (L0, 48), (D0, 48))
QUAD = 96


def tables():
    forward = np.zeros((2, PIECES, NAT), np.float32)
    quad = np.zeros((4 * QUAD, NAT), np.float32)
    for pair in range(2):
        lo, hi = range(0, 6), range(6, 12)
        sent_rows, kept_rows = (lo, hi) if pair == 0 else (hi, lo)
        first, mid, last = range(0, 3), range(3, 9), range(9, 12)
        sent_cols, kept_cols = (first, last) if pair == 0 else (last, first)

        def put(at, rows, cols):
            for l in range(2):
                for r in rows:
                    for c in cols:
                        forward[pair, at, (l * 12 + r) * SLAB + c] = 1
                        at += 1

        put(S0, sent_rows, mid)
        put(S0 + 72, sent_rows, kept_cols)
        put(L0 + 4, kept_rows, sent_cols)
        put(D0 + 12, sent_rows, sent_cols)
        put(K0 + 8, kept_rows, mid)
        put(C0, kept_rows, kept_cols)
    for l in range(2):
        for r in range(12):
            for c in range(12):
                q = (r % 2) + 2 * (c % 2)
                quad[q * QUAD + (l * 6 + r // 2) * 8 + c // 2, (l * 12 + r) * SLAB + c] = 1
    back = np.stack([np.concatenate([f.T, quad @ f.T], 0) for f in forward])
    return forward.astype(BF16), back.astype(BF16), quad.astype(BF16)


def dot(a, b):
    return jnp.dot(a, b, preferred_element_type=F32)


def kernel(
    fine_ref, ngain_ref, qkvw_ref, projw_ref, mgain_ref, shard_ref, fwd_t_ref, back_t_ref, quad_t_ref,
    out_ref, coarse_ref,
    xin, xraw, xn, fwd, rx, xw, qs, ks, vs, att, bsend, back, xquad, mask, mn, wbuf,
    qkvw, projw, fwd_t, back_t, quad_t, send, recv, local,
):
    ny = lax.axis_size("lat") // 2
    nlat, nlon = lax.axis_size("lat"), lax.axis_size("lon")
    lat, lon = lax.axis_index("lat"), lax.axis_index("lon")
    y, m = lat % ny, lat // ny
    gx, gk, core = lon // 8, (lon // 2) % 4, lon % 2
    up, down = (lat + nlat - 1) % nlat, (lat + 1) % nlat
    left, right = (lon + nlon - 1) % nlon, (lon + 1) % nlon

    xm, xp, xo = (gx + 3) % 4, (gx + 1) % 4, (gx + 2) % 4
    ko = (gk + 3 + 2 * m) % 4
    ki = (gk + 1 + 2 * m) % 4
    kf = (gk + 2) % 4
    olat = (1 - m) * ny + y
    dev_xp = (lat, xp * 8 + gk * 2 + core)
    dev_xm = (lat, xm * 8 + gk * 2 + core)
    dev_o = (olat, gx * 8 + ko * 2 + core)
    dev_i = (olat, lon)
    dev_s = (lat, lon + 1 - 2 * core)
    to = (((up, lon), (lat, left), (up, left)), ((down, lon), (lat, right), (down, right)))
    frm = (to[1], to[0])

    copies = []

    def load(src, dst):
        copy = pltpu.make_async_copy(src, dst, local.at[len(copies)])
        copy.start()
        copies.append(copy)
        return copy

    load_x = load(fine_ref, xin)
    load_ft = load(fwd_t_ref, fwd_t)
    load_qt = load(quad_t_ref, quad_t)
    load_qkv = load(qkvw_ref, qkvw)
    load_proj = load(projw_ref, projw)
    load_bt = load(back_t_ref, back_t)
    load_own = load(shard_ref, wbuf.at[lon])

    barrier = pltpu.get_barrier_semaphore()
    partners = [*to[0], *to[1], dev_xp, dev_xm, dev_o, dev_i, dev_s]
    for device in partners:
        pl.semaphore_signal(barrier, inc=1, device_id=device, device_id_type=MESH)
    pl.semaphore_wait(barrier, len(partners))

    started = []

    def push(src, dst, ident, device):
        copy = pltpu.make_async_remote_copy(
            src_ref=src, dst_ref=dst, send_sem=send.at[ident], recv_sem=recv.at[ident],
            device_id=device, device_id_type=MESH,
        )
        copy.start()
        started.append(copy)

    def arrived(dst, ident, device):
        pltpu.make_async_remote_copy(
            src_ref=dst, dst_ref=dst, send_sem=send.at[ident], recv_sem=recv.at[ident],
            device_id=device, device_id_type=MESH,
        ).wait_recv()

    def slot(x, k, first=0, rows=64, c=core):
        return wbuf.at[x * 8 + k * 2 + c, pl.ds(first, rows)]

    def forward(ident, x, k, first, rows, device):
        push(slot(x, k, first, rows), slot(x, k, first, rows), ident, device)

    def got(ident, x, k, first, rows, device):
        arrived(slot(x, k, first, rows), ident, device)

    siblings = []

    def sibling(x, k, first, rows):
        ident = 32 + len(siblings)
        siblings.append((ident, x, k, first, rows))
        forward(ident, x, k, first, rows, dev_s)

    def half(base, size, index):
        return pl.multiple_of(base + size * index, 16)

    def h1(ui, step, x):
        ident = 8 + 4 * ui + step
        if step == 0:
            forward(ident, x, gk, 0, 32, dev_o)
        elif step == 1:
            got(ident - 1, x, ko, 0, 32, dev_o)
            forward(ident, x, ko, 0, 32, dev_i)
            sibling(x, ko, 0, 32)
        elif step == 2:
            got(ident - 1, x, ki, 0, 32, dev_i)
            forward(ident, x, ki, half(0, 16, 1 - m), 16, dev_o)
            sibling(x, ki, 0, 32)
        elif step == 3:
            got(ident - 1, x, kf, half(0, 16, m), 16, dev_o)
            forward(ident, x, kf, half(0, 16, m), 16, dev_i)
        else:
            got(ident - 1, x, kf, half(0, 16, 1 - m), 16, dev_i)
            sibling(x, kf, 0, 32)

    def h2(vi, step, k):
        ident = 20 + 4 * vi
        if step == 0:
            forward(ident, gx, k, 32, 32, dev_xp)
            forward(ident + 1, gx, k, 32, 32, dev_xm)
        elif step == 1:
            got(ident, xm, k, 32, 32, dev_xm)
            forward(ident + 2, xm, k, 32, 16, dev_xp)
            sibling(xm, k, 32, 32)
            got(ident + 1, xp, k, 32, 32, dev_xp)
            forward(ident + 3, xp, k, 48, 16, dev_xm)
            sibling(xp, k, 32, 32)
        else:
            got(ident + 2, xo, k, 32, 16, dev_xm)
            got(ident + 3, xo, k, 48, 16, dev_xp)
            sibling(xo, k, 32, 32)

    def gather(stage):
        if stage == 0:
            for ident, device in ((0, dev_xp), (1, dev_xm), (2, dev_o)):
                push(shard_ref, slot(gx, gk), ident, device)
            siblings.append((32, gx, gk, 0, 64))
            push(shard_ref, slot(gx, gk), 32, dev_s)
        elif stage == 1:
            got(0, xm, gk, 0, 64, dev_xm)
            forward(3, xm, gk, 0, 32, dev_xp)
            h1(0, 0, xm)
            sibling(xm, gk, 0, 64)
            got(1, xp, gk, 0, 64, dev_xp)
            forward(4, xp, gk, 32, 32, dev_xm)
            h1(1, 0, xp)
            sibling(xp, gk, 0, 64)
            got(2, gx, ko, 0, 64, dev_o)
            forward(5, gx, ko, 0, 64, dev_i)
            h2(0, 0, ko)
            sibling(gx, ko, 0, 64)
        elif stage == 2:
            got(3, xo, gk, 0, 32, dev_xm)
            h1(2, 0, xo)
            got(4, xo, gk, 32, 32, dev_xp)
            sibling(xo, gk, 0, 64)
            got(5, gx, ki, 0, 64, dev_i)
            forward(6, gx, ki, half(0, 32, 1 - m), 32, dev_o)
            h2(1, 0, ki)
            sibling(gx, ki, 0, 64)
        elif stage == 3:
            h1(0, 1, xm)
            h1(1, 1, xp)
            h2(0, 1, ko)
            got(6, gx, kf, half(0, 32, m), 32, dev_o)
            forward(7, gx, kf, half(0, 32, m), 32, dev_i)
        elif stage == 4:
            got(7, gx, kf, half(0, 32, 1 - m), 32, dev_i)
            h2(2, 0, kf)
            sibling(gx, kf, 0, 64)
            h1(2, 1, xo)
            h2(1, 1, ki)
        elif stage == 5:
            h1(0, 2, xm)
            h1(1, 2, xp)
            h2(0, 2, ko)
        elif stage == 6:
            h1(2, 2, xo)
            h1(0, 3, xm)
            h1(1, 3, xp)
            h2(2, 1, kf)
            h2(1, 2, ki)
        elif stage == 7:
            h1(0, 4, xm)
            h1(1, 4, xp)
            h1(2, 3, xo)
            h2(2, 2, kf)
        else:
            h1(2, 4, xo)

    gather(0)

    xn[...] = jnp.zeros_like(xn)
    xraw[...] = jnp.zeros_like(xraw)
    gain = ngain_ref[...]
    load_x.wait()
    load_ft.wait()
    for pair in range(2):
        for l, level in enumerate(LEVELS[pair]):
            for r in range(0, 12, 4):
                raw = xin[level, r : r + 4]
                values = raw.astype(F32)
                mean = jnp.mean(values, -1, keepdims=True)
                centered = values - mean
                spread = jnp.mean(centered * centered, -1, keepdims=True)
                normed = centered * lax.rsqrt(spread + 1e-05) * gain
                xn[pair, l, r : r + 4, 0:12, :] = normed.astype(BF16)
                xraw[pair, l, r : r + 4, 0:12, :] = raw
        fwd[pair] = dot(fwd_t[pair], xn[pair].reshape(NAT, WIDTH)).astype(BF16)
        for i, (at, rows) in enumerate(SENT):
            push(fwd.at[pair, pl.ds(at, rows)], rx.at[pair, pl.ds(at, rows)], 57 + 3 * pair + i, to[pair][i])

    gather(1)

    for pair in range(2):
        wrap = (lat == (nlat - 1 if pair == 0 else 0)).astype(jnp.int32)
        for w in range(2):
            codes = []
            for dim in range(2):
                at = lax.broadcasted_iota(jnp.int32, (WIN, WIN), dim)
                other = jnp.where(at < 72, 1, 0)
                level = ((at * 57) >> (11 - w)) & 1
                codes.append(other * wrap + 2 * level * pair)
            mask[pair, w] = jnp.where(codes[0] == codes[1], 1.0, 0.0)

    gather(2)

    load_qt.wait()
    for pair in range(2):
        xquad[pair] = dot(quad_t[...], xraw[pair].reshape(NAT, WIDTH)).astype(BF16)

    gather(3)

    lane = lax.broadcasted_iota(jnp.int32, (1, 128), 1)
    low = jnp.where(lane < 64, 1.0, 0.0).astype(BF16)
    high = jnp.where(lane < 64, 0.0, 1.0).astype(BF16)

    def attend(w):
        def one(p, carry):
            lanes = pl.ds(pl.multiple_of(p * 128, 128), 128)
            q = qs[w, :, lanes]
            both = jnp.concatenate([q * low, q * high], 0)
            scores = lax.dot_general(
                both, ks[w, :, lanes], (((1,), (1,)), ((), ())), preferred_element_type=F32
            ).reshape(2, WIN, WIN)
            return scores, lanes

        def body(p, carry):
            scores, lanes = one(p, carry)
            same = mask[pair, w] > 0.5
            scores = jnp.where(same[None], scores, -1e30)
            top = jnp.max(scores, -1, keepdims=True)
            expo = jnp.exp(scores - top).astype(BF16).reshape(2 * WIN, WIN)
            v = vs[w, :, lanes]
            result = dot(expo, jnp.concatenate([v, jnp.ones_like(v)], 1))
            result = result[:, :128] / result[:, 128:]
            att[w, :, lanes] = jnp.where(lane < 64, result[:WIN], result[WIN:]).astype(BF16)
            return carry

        lax.fori_loop(0, PAIRS, body, 0)

    def seam(a, b, rows):
        keep = lax.broadcasted_iota(jnp.int32, (16, WIDTH), 0) < rows
        return jnp.where(keep, a.astype(F32), b.astype(F32)).astype(BF16)

    for pair in range(2):
        for i, (at, rows) in enumerate(SENT):
            arrived(rx.at[pair, pl.ds(at, rows)], 57 + 3 * pair + i, frm[pair][i])
        s, l, d = rx.at[pair, pl.ds(S0, 112)], rx.at[pair, pl.ds(L0, 48)], rx.at[pair, pl.ds(D0, 48)]
        kb, kc = fwd.at[pair, pl.ds(K0, 80)], fwd.at[pair, pl.ds(C0, 48)]
        xw[0:64] = s[0:64]
        xw[64:80] = seam(s[64:80], kb[0:16], 8)
        xw[80:144] = kb[16:80]
        xw[144:176] = kc[0:32]
        xw[176:192] = seam(kc[32:48], l[0:16], 4)
        xw[192:208] = l[16:32]
        xw[208:224] = seam(l[32:48], s[64:80], 8)
        xw[224:240] = s[80:96]
        xw[240:256] = seam(s[96:112], d[0:16], 12)
        xw[256:288] = d[16:48]
        if pair == 0:
            load_qkv.wait()
        tokens = xw[...]
        qs[...] = (dot(tokens, qkvw[:, :WIDTH]) * 0.125).astype(BF16).reshape(2, WIN, WIDTH)
        ks[...] = dot(tokens, qkvw[:, WIDTH : 2 * WIDTH]).astype(BF16).reshape(2, WIN, WIDTH)
        vs[...] = dot(tokens, qkvw[:, 2 * WIDTH :]).astype(BF16).reshape(2, WIN, WIDTH)
        if pair == 0:
            gather(4)
        attend(0)
        gather(5 if pair == 0 else 7)
        attend(1)
        if pair == 0:
            load_proj.wait()
        branch = dot(att[...].reshape(2 * WIN, WIDTH), projw[...])
        bsend[pair, 0:112] = jnp.concatenate([branch[0:72], branch[216:256]], 0).astype(BF16)
        bsend[pair, 112:160] = branch[176:224].astype(BF16)
        bsend[pair, 160:208] = branch[240:288].astype(BF16)
        back[pair, 208:288] = branch[64:144].astype(BF16)
        back[pair, 288:336] = branch[144:192].astype(BF16)
        for i, (at, rows) in enumerate(SENT):
            push(bsend.at[pair, pl.ds(at, rows)], back.at[pair, pl.ds(at, rows)], 63 + 3 * pair + i, frm[pair][i])
        gather(6 if pair == 0 else 8)

    load_bt.wait()
    mgain = mgain_ref[...]
    for pair in range(2):
        for i, (at, rows) in enumerate(SENT):
            arrived(back.at[pair, pl.ds(at, rows)], 63 + 3 * pair + i, to[pair][i])
        pieces = back[pair]
        grid = dot(back_t[pair, :NAT], pieces).reshape(2, 12, SLAB, WIDTH)
        for l, level in enumerate(LEVELS[pair]):
            out = xraw[pair, l].astype(F32) + grid[l]
            out_ref[level] = out[:, 0:12].astype(BF16)
        quads = dot(back_t[pair, NAT:], pieces) + xquad[pair].astype(F32)
        quads = quads.astype(BF16).astype(F32).reshape(4, QUAD, WIDTH)
        mean = jnp.sum(jnp.sum(quads, 0), -1, keepdims=True) / (4 * WIDTH)
        centered = quads - mean
        spread = jnp.sum(jnp.sum(centered * centered, 0), -1, keepdims=True) / (4 * WIDTH)
        scale = lax.rsqrt(spread + 1e-05)
        for q in range(4):
            cols = slice(q * WIDTH, (q + 1) * WIDTH)
            mn[pair * QUAD : (pair + 1) * QUAD, cols] = (centered[q] * scale * mgain[cols]).astype(BF16)

    load_own.wait()
    for ident, x, k, first, rows in siblings:
        arrived(slot(x, k, first, rows, 1 - core), ident, dev_s)

    def merge(n, carry):
        lanes = pl.ds(pl.multiple_of(n * 256, 256), 256)
        weight = wbuf[:, :, lanes].reshape(4 * WIDTH, 256)
        merged = dot(mn[...], weight).reshape(2, 2, 6, 8, 256)
        for pair in range(2):
            for l, level in enumerate(LEVELS[pair]):
                coarse_ref[level, :, :, lanes] = merged[pair, l][:, 0:6].astype(BF16)
        return carry

    lax.fori_loop(0, 4, merge, 0)

    for copy in started:
        copy.wait_send()


def local(fine_in, norm_gain, qkv_weight, proj_weight, merge_gain, merge_weight, fwd_t, back_t, quad_t):
    anywhere = pl.BlockSpec(memory_space=pl.ANY)
    vmem = pl.BlockSpec(memory_space=pltpu.VMEM)
    scratch = [
        ((4, 12, 12, WIDTH), BF16),
        ((2, 2, 12, SLAB, WIDTH), BF16),
        ((2, 2, 12, SLAB, WIDTH), BF16),
        ((2, PIECES, WIDTH), BF16),
        ((2, 208, WIDTH), BF16),
        ((2 * WIN, WIDTH), BF16),
        ((2, WIN, WIDTH), BF16),
        ((2, WIN, WIDTH), BF16),
        ((2, WIN, WIDTH), BF16),
        ((2, WIN, WIDTH), BF16),
        ((2, 208, WIDTH), BF16),
        ((2, PIECES, WIDTH), BF16),
        ((2, 4 * QUAD, WIDTH), BF16),
        ((2, 2, WIN, WIN), F32),
        ((2 * QUAD, 4 * WIDTH), BF16),
        ((32, 64, 2 * WIDTH), BF16),
        ((WIDTH, 3 * WIDTH), BF16),
        ((WIDTH, WIDTH), BF16),
        (fwd_t.shape, BF16),
        (back_t.shape, BF16),
        (quad_t.shape, BF16),
    ]
    return pl.pallas_call(
        kernel,
        out_shape=(
            jax.ShapeDtypeStruct((4, 12, 12, WIDTH), BF16),
            jax.ShapeDtypeStruct((4, 6, 6, 2 * WIDTH), BF16),
        ),
        in_specs=[anywhere, vmem, anywhere, anywhere, vmem, anywhere, anywhere, anywhere, anywhere],
        out_specs=(vmem, vmem),
        scratch_shapes=[pltpu.VMEM(shape, dtype) for shape, dtype in scratch]
        + [pltpu.SemaphoreType.DMA((69,)), pltpu.SemaphoreType.DMA((69,)), pltpu.SemaphoreType.DMA((7,))],
        compiler_params=pltpu.CompilerParams(
            collective_id=0, has_side_effects=True, vmem_limit_bytes=56 * 1024 * 1024
        ),
        name="swin_block",
    )(fine_in, norm_gain, qkv_weight, proj_weight, merge_gain, merge_weight, fwd_t, back_t, quad_t)


def solution(mesh):
    placed = (P(None, "lat", "lon", None), P(), P(), P(), P(), P("lon", None), P(), P(), P())
    run = jax.shard_map(
        local,
        mesh=mesh,
        in_specs=placed,
        out_specs=(P(None, "lat", "lon", None), P(None, "lat", "lon", None)),
        check_vma=False,
    )

    def whole(*arrays):
        return run(*arrays, *(jnp.asarray(table) for table in tables()))

    return whole
```

```python
import functools

import jax
import jax.numpy as jnp
import numpy as np
from jax import lax
from jax.experimental import pallas as pl
from jax.experimental.pallas import tpu as pltpu
from jax.sharding import PartitionSpec as P

MESH = pl.DeviceIdType.MESH
BF16 = jnp.bfloat16
F32 = jnp.float32

WIDTH = 512
PAIRS = 4
WIN = 144
LEVELS = ((1, 2), (3, 0))
TILE = 576
SENT = ((0, 80), (80, 48), (128, 48), (176, 48))
OWN = 224
PIECES = 352


def tables():
    forward = np.zeros((2, PIECES, TILE), np.float32)
    quad = np.zeros((2, 288, TILE), np.float32)
    order = np.zeros((144, 144), np.float32)
    for pair in range(2):
        lo, hi = range(0, 6), range(6, 12)
        sent_rows, kept_rows = (lo, hi) if pair == 0 else (hi, lo)
        first, mid, last = range(0, 3), range(3, 9), range(9, 12)
        sent_cols, kept_cols = (first, last) if pair == 0 else (last, first)

        def put(at, rows, cols):
            for level in LEVELS[pair]:
                for r in rows:
                    for c in cols:
                        forward[pair, at, (r * 12 + c) * 4 + level] = 1
                        at += 1

        put(0, sent_rows, mid)
        put(80 + 8, sent_rows, kept_cols)
        put(128 + 4, kept_rows, sent_cols)
        put(176 + 12, sent_rows, sent_cols)
        put(OWN + 8, kept_rows, mid)
        put(OWN + 80, kept_rows, kept_cols)
        for l, level in enumerate(LEVELS[pair]):
            for r in range(12):
                for c in range(12):
                    q, at = (r % 2) + 2 * (c % 2), (r // 2) * 6 + c // 2
                    quad[pair, q * 72 + l * 36 + at, (r * 12 + c) * 4 + level] = 1
                    order[at * 4 + level, pair * 72 + l * 36 + at] = 1
    back = np.concatenate([forward[0].T, forward[1].T], 1)
    backq = np.stack([quad[pair] @ forward[pair].T for pair in range(2)])
    return [table.astype(BF16) for table in (forward, back, backq, quad, order)]


def dot(a, b):
    return jnp.dot(a, b, preferred_element_type=F32)


def kernel(
    fine_ref, ngain_ref, qkvw_ref, projw_ref, mgain_ref, shard_ref, fwd_ref, back_ref, backq_ref, quad_ref, order_ref,
    out_ref, coarse_ref,
    xin, xraw, xn, fwd, rx, xw, att, bsend, back, xquad, mask, mn, merged, out, wbuf,
    qkvw, projw, fwd_t, back_t, backq_t, quad_t, order_t, send, recv, local,
):
    ny = lax.axis_size("lat") // 2
    nlat, nlon = lax.axis_size("lat"), lax.axis_size("lon")
    lat, lon = lax.axis_index("lat"), lax.axis_index("lon")
    y, m = lat % ny, lat // ny
    gx, gk, core = lon // 8, (lon // 2) % 4, lon % 2
    up, down = (lat + nlat - 1) % nlat, (lat + 1) % nlat
    left, right = (lon + nlon - 1) % nlon, (lon + 1) % nlon

    xm, xp, xo = (gx + 3) % 4, (gx + 1) % 4, (gx + 2) % 4
    ko = (gk + 3 + 2 * m) % 4
    ki = (gk + 1 + 2 * m) % 4
    kf = (gk + 2) % 4
    olat = (1 - m) * ny + y
    dev_xp = (lat, xp * 8 + gk * 2 + core)
    dev_xm = (lat, xm * 8 + gk * 2 + core)
    dev_o = (olat, gx * 8 + ko * 2 + core)
    dev_i = (olat, lon)
    dev_f = (lat, gx * 8 + ki * 2 + core)
    dev_g = (lat, gx * 8 + ko * 2 + core)
    dev_s = (lat, lon + 1 - 2 * core)
    to = (((up, lon), (up, lon), (lat, left), (up, left)), ((down, lon), (down, lon), (lat, right), (down, right)))
    frm = (to[1], to[0])

    barrier = pltpu.get_barrier_semaphore()
    partners = [*to[0][1:], *to[1][1:], dev_xp, dev_xm, dev_o, dev_i, dev_f, dev_g, dev_s]
    for device in partners:
        pl.semaphore_signal(barrier, inc=1, device_id=device, device_id_type=MESH)

    copies = []

    def load(src, dst):
        copy = pltpu.make_async_copy(src, dst, local.at[len(copies)])
        copy.start()
        copies.append(copy)
        return copy

    load_x = load(fine_ref, xin)
    load_f = load(fwd_ref, fwd_t)
    load_qkv = load(qkvw_ref, qkvw)
    load_q = load(quad_ref, quad_t)
    load_proj = load(projw_ref, projw)
    load_bq = load(backq_ref, backq_t)
    load_b = load(back_ref, back_t)
    load_order = load(order_ref, order_t)
    load_own = load(shard_ref, wbuf.at[lon])

    started = []

    def push(src, dst, ident, device):
        copy = pltpu.make_async_remote_copy(
            src_ref=src, dst_ref=dst, send_sem=send.at[ident], recv_sem=recv.at[ident],
            device_id=device, device_id_type=MESH,
        )
        copy.start()
        started.append(copy)

    def arrived(dst, ident, device):
        pltpu.make_async_remote_copy(
            src_ref=dst, dst_ref=dst, send_sem=send.at[ident], recv_sem=recv.at[ident],
            device_id=device, device_id_type=MESH,
        ).wait_recv()

    def slot(x, k, first=0, rows=64, c=core):
        return wbuf.at[x * 8 + k * 2 + c, pl.ds(first, rows)]

    def forward(ident, x, k, first, rows, device):
        push(slot(x, k, first, rows), slot(x, k, first, rows), ident, device)

    def got(ident, x, k, first, rows, device):
        arrived(slot(x, k, first, rows), ident, device)

    siblings = []

    def sibling(x, k, first, rows):
        ident = 25 + len(siblings)
        siblings.append((ident, x, k, first, rows))
        forward(ident, x, k, first, rows, dev_s)

    h1_ids, h2_ids = 7, 13
    sides = ((xm, dev_xm, dev_xp), (xp, dev_xp, dev_xm))

    def line(ident, k, first, rows):
        forward(ident, gx, k, first, rows, dev_xp)
        forward(ident + 1, gx, k, first, rows, dev_xm)

    def relay(ident, side, k, first, rows):
        x, source, target = sides[side]
        got(ident + side, x, k, first, rows, source)
        forward(ident + 2 + side, x, k, first + side * rows // 2, rows // 2, target)

    def far(ident, k, first, rows):
        for side, (_, source, _) in enumerate(sides):
            got(ident + 2 + side, xo, k, first + side * rows // 2, rows // 2, source)

    def gather(stage):
        if stage == 0:
            for ident, device in ((4, dev_o), (0, dev_xp), (1, dev_xm)):
                push(shard_ref, slot(gx, gk), ident, device)
            siblings.append((25, gx, gk, 0, 64))
            push(shard_ref, slot(gx, gk), 25, dev_s)
        elif stage == 1:
            got(4, gx, ko, 0, 64, dev_o)
            forward(5, gx, ko, 0, 64, dev_i)
            forward(6, gx, ko, 0, 64, dev_f)
            line(h2_ids, ko, 32, 32)
            sibling(gx, ko, 0, 64)
        elif stage == 2:
            for side in range(2):
                x = sides[side][0]
                relay(0, side, gk, 0, 64)
                forward(h1_ids + 2 * side, x, gk, 0, 32, dev_o)
                sibling(x, gk, 0, 64)
        elif stage == 3:
            got(5, gx, ki, 0, 64, dev_i)
            line(h2_ids + 4, ki, 32, 32)
            sibling(gx, ki, 0, 64)
            got(6, gx, kf, 0, 64, dev_g)
            line(h2_ids + 8, kf, 0, 64)
            sibling(gx, kf, 0, 64)
        elif stage == 4:
            far(0, gk, 0, 64)
            forward(h1_ids + 4, xo, gk, 0, 32, dev_o)
            sibling(xo, gk, 0, 64)
            for side in range(2):
                x = sides[side][0]
                relay(h2_ids, side, ko, 32, 32)
                got(h1_ids + 2 * side, x, ko, 0, 32, dev_o)
                forward(h1_ids + 2 * side + 1, x, ko, 0, 32, dev_i)
                sibling(x, ko, 0, 64)
        elif stage == 5:
            for side in range(2):
                relay(h2_ids + 4, side, ki, 32, 32)
            for side in range(2):
                relay(h2_ids + 8, side, kf, 0, 64)
                sibling(sides[side][0], kf, 0, 64)
            far(h2_ids, ko, 32, 32)
            got(h1_ids + 4, xo, ko, 0, 32, dev_o)
            forward(h1_ids + 5, xo, ko, 0, 32, dev_i)
            sibling(xo, ko, 0, 64)
        else:
            for side in range(2):
                x = sides[side][0]
                got(h1_ids + 2 * side + 1, x, ki, 0, 32, dev_i)
                sibling(x, ki, 0, 64)
            far(h2_ids + 8, kf, 0, 64)
            sibling(xo, kf, 0, 64)
            far(h2_ids + 4, ki, 32, 32)
            got(h1_ids + 5, xo, ki, 0, 32, dev_i)
            sibling(xo, ki, 0, 64)

    gain = ngain_ref[...]
    load_x.wait()
    for at in range(0, TILE, 64):
        raw = xin[at // 4 : at // 4 + 16].astype(F32).reshape(64, WIDTH)
        xraw[at : at + 64] = raw.astype(BF16)
        mean = jnp.mean(raw, -1, keepdims=True)
        centered = raw - mean
        spread = jnp.mean(centered * centered, -1, keepdims=True)
        xn[at : at + 64] = (centered * lax.rsqrt(spread + 1e-05) * gain).astype(BF16)
    load_f.wait()
    for pair in range(2):
        fwd[pair] = dot(fwd_t[pair], xn[...]).astype(BF16)
        if pair == 0:
            pl.semaphore_wait(barrier, len(partners))
        for i, (at, rows) in enumerate(SENT):
            push(fwd.at[pair, pl.ds(at, rows)], rx.at[pair, pl.ds(at, rows)], 41 + 4 * pair + i, to[pair][i])

    gather(0)

    for pair in range(2):
        wrap = (lat == (nlat - 1 if pair == 0 else 0)).astype(jnp.int32)
        for w in range(2):
            codes = []
            for dim in range(2):
                at = lax.broadcasted_iota(jnp.int32, (WIN, WIN), dim)
                other = jnp.where(at < 72, 1, 0)
                level = ((at * 57) >> (11 - w)) & 1
                codes.append(other * wrap + 2 * level * pair)
            mask[pair, w] = jnp.where(codes[0] == codes[1], 1.0, 0.0)

    load_q.wait()
    for pair in range(2):
        xquad[pair] = dot(quad_t[pair], xraw[...])

    gather(1)

    lane = lax.broadcasted_iota(jnp.int32, (1, 128), 1)
    low = jnp.where(lane < 64, 1.0, 0.0).astype(BF16)
    high = jnp.where(lane < 64, 0.0, 1.0).astype(BF16)

    def attend(pair, w, tokens):
        q = (dot(tokens, qkvw[:, :WIDTH]) * 0.125).astype(BF16)
        k = dot(tokens, qkvw[:, WIDTH : 2 * WIDTH]).astype(BF16)
        v = dot(tokens, qkvw[:, 2 * WIDTH :]).astype(BF16)
        same = mask[pair, w] > 0.5
        ones = jnp.ones((WIN, 128), BF16)
        for p in range(PAIRS):
            cols = slice(p * 128, (p + 1) * 128)
            both = jnp.concatenate([q[:, cols] * low, q[:, cols] * high], 0)
            scores = lax.dot_general(both, k[:, cols], (((1,), (1,)), ((), ())), preferred_element_type=F32)
            scores = jnp.where(same[None], scores.reshape(2, WIN, WIN), -1e30)
            top = jnp.max(scores, -1, keepdims=True)
            expo = jnp.exp(scores - top).astype(BF16).reshape(2 * WIN, WIN)
            result = dot(expo, jnp.concatenate([v[:, cols], ones], 1))
            result = result[:, :128] / result[:, 128:]
            att[pair, w, :, cols] = jnp.where(lane < 64, result[:WIN], result[WIN:]).astype(BF16)
        return dot(att[pair, w], projw[...]).astype(BF16)

    def send_back(pair, i):
        at, rows = SENT[i]
        push(bsend.at[pair, pl.ds(at, rows)], back.at[pair, pl.ds(at, rows)], 49 + 4 * pair + i, frm[pair][i])

    def await_piece(pair, i):
        at, rows = SENT[i]
        arrived(rx.at[pair, pl.ds(at, rows)], 41 + 4 * pair + i, frm[pair][i])

    load_qkv.wait()
    load_proj.wait()
    for pair in range(2):
        await_piece(pair, 0)
        s, own = rx.at[pair, pl.ds(0, 80)], fwd.at[pair, pl.ds(OWN, 80)]
        x = xw.at[pair, 0]
        x[0:64] = s[0:64]
        x[64:80] = s[64:80] + own[0:16]
        x[80:144] = own[16:80]
        branch = attend(pair, 0, x[...])
        bsend[pair, 0:80] = branch[0:80]
        send_back(pair, 0)
        back[pair, OWN : OWN + 80] = branch[64:144]
        if pair == 0:
            gather(2)

    for pair in range(2):
        for i in range(1, 4):
            await_piece(pair, i)
        s, l, d = (rx.at[pair, pl.ds(*SENT[i])] for i in range(1, 4))
        own = fwd.at[pair, pl.ds(OWN + 80, 48)]
        x = xw.at[pair, 1]
        x[0:32] = own[0:32]
        x[32:48] = own[32:48] + l[0:16]
        x[48:64] = l[16:32]
        x[64:80] = l[32:48] + s[0:16]
        x[80:96] = s[16:32]
        x[96:112] = s[32:48] + d[0:16]
        x[112:144] = d[16:48]
        branch = attend(pair, 1, x[...])
        bsend[pair, 80:128] = branch[64:112]
        bsend[pair, 128:176] = branch[32:80]
        bsend[pair, 176:224] = branch[96:144]
        for i in range(1, 4):
            send_back(pair, i)
        back[pair, OWN + 80 : PIECES] = branch[0:48]

    gather(3)
    gather(4)
    load_bq.wait()
    mgain = mgain_ref[...]
    for pair in range(2):
        for i, (at, rows) in enumerate(SENT):
            arrived(back.at[pair, pl.ds(at, rows)], 49 + 4 * pair + i, to[pair][i])
        if pair == 1:
            gather(5)
        quads = dot(backq_t[pair], back[pair]) + xquad[pair]
        quads = quads.astype(BF16).astype(F32).reshape(4, 72, WIDTH)
        mean = jnp.sum(jnp.sum(quads, 0), -1, keepdims=True) / (4 * WIDTH)
        centered = quads - mean
        spread = jnp.sum(jnp.sum(centered * centered, 0), -1, keepdims=True) / (4 * WIDTH)
        scale = lax.rsqrt(spread + 1e-05)
        for q in range(4):
            cols = slice(q * WIDTH, (q + 1) * WIDTH)
            mn[pair * 72 : (pair + 1) * 72, cols] = (centered[q] * scale * mgain[cols]).astype(BF16)

    load_b.wait()
    pieces = back[...].reshape(2 * PIECES, WIDTH)
    for at in range(0, TILE, 192):
        rows = dot(back_t[at : at + 192], pieces) + xraw[at : at + 192].astype(F32)
        out[at // 4 : at // 4 + 48] = rows.reshape(48, 4, WIDTH).astype(BF16)
    store_out = pltpu.make_async_copy(out, out_ref, local.at[9])
    store_out.start()

    gather(6)
    load_own.wait()
    load_order.wait()
    for ident, x, k, first, rows in siblings:
        arrived(slot(x, k, first, rows, 1 - core), ident, dev_s)

    def merge(n, carry):
        lanes = pl.ds(pl.multiple_of(n * 256, 256), 256)
        weight = wbuf[:, :, lanes].reshape(4 * WIDTH, 256)
        result = dot(mn[...], weight).astype(BF16)
        merged[:, :, lanes] = dot(order_t[...], result).reshape(36, 4, 256).astype(BF16)
        return carry

    lax.fori_loop(0, 4, merge, 0, unroll=True)
    store_merged = pltpu.make_async_copy(merged, coarse_ref, local.at[10])
    store_merged.start()

    for copy in started:
        copy.wait_send()
    store_out.wait()
    store_merged.wait()


def place(fine_ref, merged_ref, out_ref, coarse_ref, out, merged, came, left):
    parts = []
    for source, held, target in ((fine_ref, out, out_ref), (merged_ref, merged, coarse_ref)):
        rows = source.shape[0] // 4
        for i in range(4):
            at, part = pl.ds(i * rows, rows), len(parts)
            enter = pltpu.make_async_copy(source.at[at], held.at[at], came.at[part])
            enter.start()
            parts.append((enter, pltpu.make_async_copy(held.at[at], target.at[at], left.at[part])))
    for enter, leave in parts:
        enter.wait()
        leave.start()
    for _, leave in parts:
        leave.wait()


def local(fine_in, norm_gain, qkv_weight, proj_weight, merge_gain, merge_weight, *constants):
    anywhere = pl.BlockSpec(memory_space=pl.ANY)
    vmem = pl.BlockSpec(memory_space=pltpu.VMEM)
    scratch = [
        ((144, 4, WIDTH), BF16),
        ((TILE, WIDTH), BF16),
        ((TILE, WIDTH), BF16),
        ((2, PIECES, WIDTH), BF16),
        ((2, OWN, WIDTH), BF16),
        ((2, 2, WIN, WIDTH), BF16),
        ((2, 2, WIN, WIDTH), BF16),
        ((2, OWN, WIDTH), BF16),
        ((2, PIECES, WIDTH), BF16),
        ((2, 288, WIDTH), F32),
        ((2, 2, WIN, WIN), F32),
        ((144, 4 * WIDTH), BF16),
        ((36, 4, 2 * WIDTH), BF16),
        ((144, 4, WIDTH), BF16),
        ((32, 64, 2 * WIDTH), BF16),
        ((WIDTH, 3 * WIDTH), BF16),
        ((WIDTH, WIDTH), BF16),
        *((table.shape, BF16) for table in constants),
    ]
    tile = fine_in.transpose(1, 2, 0, 3).reshape(144, 4, WIDTH)
    out, coarse = pl.pallas_call(
        kernel,
        out_shape=(
            jax.ShapeDtypeStruct((144, 4, WIDTH), BF16),
            jax.ShapeDtypeStruct((36, 4, 2 * WIDTH), BF16),
        ),
        in_specs=[anywhere, vmem, anywhere, anywhere, vmem, anywhere] + [anywhere] * len(constants),
        out_specs=(anywhere, anywhere),
        scratch_shapes=[pltpu.VMEM(shape, dtype) for shape, dtype in scratch]
        + [pltpu.SemaphoreType.DMA((57,)), pltpu.SemaphoreType.DMA((57,)), pltpu.SemaphoreType.DMA((11,))],
        compiler_params=pltpu.CompilerParams(
            collective_id=0, has_side_effects=True, vmem_limit_bytes=56 * 1024 * 1024
        ),
        name="swin_block",
    )(tile, norm_gain, qkv_weight, proj_weight, merge_gain, merge_weight, *constants)
    fine_out, coarse = pl.pallas_call(
        place,
        out_shape=(jax.ShapeDtypeStruct(out.shape, BF16), jax.ShapeDtypeStruct(coarse.shape, BF16)),
        in_specs=[anywhere] * 2,
        out_specs=(anywhere, anywhere),
        scratch_shapes=[
            pltpu.VMEM(out.shape, BF16),
            pltpu.VMEM(coarse.shape, BF16),
            pltpu.SemaphoreType.DMA((8,)),
            pltpu.SemaphoreType.DMA((8,)),
        ],
        name="place",
    )(out, coarse)
    return (
        fine_out.reshape(12, 12, 4, WIDTH).transpose(2, 0, 1, 3),
        coarse.reshape(6, 6, 4, 2 * WIDTH).transpose(2, 0, 1, 3),
    )


def solution(mesh):
    grid = P(None, "lat", "lon", None)
    constants = tables()
    run = jax.shard_map(
        local,
        mesh=mesh,
        in_specs=(grid, P(), P(), P(), P(), P("lon", None), *(P() for _ in constants)),
        out_specs=(grid, grid),
        check_vma=False,
    )

    def whole(*arrays):
        return run(*arrays, *(jnp.asarray(table) for table in constants))

    return whole
```

```python
import functools

import jax
import jax.numpy as jnp
import numpy as np
from jax import lax
from jax.experimental import pallas as pl
from jax.experimental.pallas import tpu as pltpu
from jax.sharding import PartitionSpec as P

MESH = pl.DeviceIdType.MESH
BF16 = jnp.bfloat16
F32 = jnp.float32

WIDTH = 512
PAIRS = 4
WIN = 144
LEVELS = ((1, 2), (3, 0))
TILE = 576
SENT = ((0, 80), (80, 48), (128, 48), (176, 48))
OWN = 224
PIECES = 352


def tables():
    forward = np.zeros((2, PIECES, TILE), np.float32)
    quad = np.zeros((2, 288, TILE), np.float32)
    order = np.zeros((144, 144), np.float32)
    for pair in range(2):
        lo, hi = range(0, 6), range(6, 12)
        sent_rows, kept_rows = (lo, hi) if pair == 0 else (hi, lo)
        first, mid, last = range(0, 3), range(3, 9), range(9, 12)
        sent_cols, kept_cols = (first, last) if pair == 0 else (last, first)

        def put(at, rows, cols):
            for level in LEVELS[pair]:
                for r in rows:
                    for c in cols:
                        forward[pair, at, (r * 12 + c) * 4 + level] = 1
                        at += 1

        put(0, sent_rows, mid)
        put(80 + 8, sent_rows, kept_cols)
        put(128 + 4, kept_rows, sent_cols)
        put(176 + 12, sent_rows, sent_cols)
        put(OWN + 8, kept_rows, mid)
        put(OWN + 80, kept_rows, kept_cols)
        for l, level in enumerate(LEVELS[pair]):
            for r in range(12):
                for c in range(12):
                    q, at = (r % 2) + 2 * (c % 2), (r // 2) * 6 + c // 2
                    quad[pair, q * 72 + l * 36 + at, (r * 12 + c) * 4 + level] = 1
                    order[at * 4 + level, pair * 72 + l * 36 + at] = 1
    back = np.concatenate([forward[0].T, forward[1].T], 1)
    backq = np.stack([quad[pair] @ forward[pair].T for pair in range(2)])
    return [table.astype(BF16) for table in (forward, back, backq, quad, order)]


def dot(a, b):
    return jnp.dot(a, b, preferred_element_type=F32)


def kernel(
    fine_ref, ngain_ref, qkvw_ref, projw_ref, mgain_ref, shard_ref, fwd_ref, back_ref, backq_ref, quad_ref, order_ref,
    out_ref, coarse_ref,
    xin, xraw, xn, fwd, rx, xw, att, bsend, back, xquad, mask, mn, merged, out, wbuf,
    qkvw, projw, fwd_t, back_t, backq_t, quad_t, order_t, send, recv, local,
):
    ny = lax.axis_size("lat") // 2
    nlat, nlon = lax.axis_size("lat"), lax.axis_size("lon")
    lat, lon = lax.axis_index("lat"), lax.axis_index("lon")
    y, m = lat % ny, lat // ny
    gx, gk, core = lon // 8, (lon // 2) % 4, lon % 2
    up, down = (lat + nlat - 1) % nlat, (lat + 1) % nlat
    left, right = (lon + nlon - 1) % nlon, (lon + 1) % nlon

    xm, xp, xo = (gx + 3) % 4, (gx + 1) % 4, (gx + 2) % 4
    ko = (gk + 3 + 2 * m) % 4
    ki = (gk + 1 + 2 * m) % 4
    kf = (gk + 2) % 4
    olat = (1 - m) * ny + y
    dev_xp = (lat, xp * 8 + gk * 2 + core)
    dev_xm = (lat, xm * 8 + gk * 2 + core)
    dev_o = (olat, gx * 8 + ko * 2 + core)
    dev_i = (olat, lon)
    dev_far = (olat, gx * 8 + kf * 2 + core)
    dev_s = (lat, lon + 1 - 2 * core)
    to = (((up, lon), (up, lon), (lat, left), (up, left)), ((down, lon), (down, lon), (lat, right), (down, right)))
    frm = (to[1], to[0])

    barrier = pltpu.get_barrier_semaphore()
    partners = [*to[0][1:], *to[1][1:], dev_xp, dev_xm, dev_o, dev_i, dev_far, dev_s]
    for device in partners:
        pl.semaphore_signal(barrier, inc=1, device_id=device, device_id_type=MESH)

    copies = []

    def load(src, dst):
        copy = pltpu.make_async_copy(src, dst, local.at[len(copies)])
        copy.start()
        copies.append(copy)
        return copy

    load_x = load(fine_ref, xin)
    load_f = load(fwd_ref, fwd_t)
    load_qkv = load(qkvw_ref, qkvw)
    load_q = load(quad_ref, quad_t)
    load_proj = load(projw_ref, projw)
    load_bq = load(backq_ref, backq_t)
    load_b = load(back_ref, back_t)
    load_order = load(order_ref, order_t)
    load_own = load(shard_ref, wbuf.at[lon])

    started = []

    def push(src, dst, ident, device):
        copy = pltpu.make_async_remote_copy(
            src_ref=src, dst_ref=dst, send_sem=send.at[ident], recv_sem=recv.at[ident],
            device_id=device, device_id_type=MESH,
        )
        copy.start()
        started.append(copy)

    def arrived(dst, ident, device):
        pltpu.make_async_remote_copy(
            src_ref=dst, dst_ref=dst, send_sem=send.at[ident], recv_sem=recv.at[ident],
            device_id=device, device_id_type=MESH,
        ).wait_recv()

    def slot(x, k, first=0, rows=64, c=core):
        return wbuf.at[x * 8 + k * 2 + c, pl.ds(first, rows)]

    def forward(ident, x, k, first, rows, device):
        push(slot(x, k, first, rows), slot(x, k, first, rows), ident, device)

    def got(ident, x, k, first, rows, device):
        arrived(slot(x, k, first, rows), ident, device)

    siblings = []

    def sibling(x, k, first, rows):
        ident = 25 + len(siblings)
        siblings.append((ident, x, k, first, rows))
        forward(ident, x, k, first, rows, dev_s)

    h1_ids, h2_ids = 7, 13
    sides = ((xm, dev_xm, dev_xp), (xp, dev_xp, dev_xm))

    def line(ident, k, first, rows):
        forward(ident, gx, k, first, rows, dev_xp)
        forward(ident + 1, gx, k, first, rows, dev_xm)

    def relay(ident, side, k, first, rows):
        x, source, target = sides[side]
        got(ident + side, x, k, first, rows, source)
        forward(ident + 2 + side, x, k, first + side * rows // 2, rows // 2, target)

    def far(ident, k, first, rows):
        for side, (_, source, _) in enumerate(sides):
            got(ident + 2 + side, xo, k, first + side * rows // 2, rows // 2, source)

    def gather(stage):
        if stage == 0:
            for ident, device in ((4, dev_o), (0, dev_xp), (1, dev_xm)):
                push(shard_ref, slot(gx, gk), ident, device)
            siblings.append((25, gx, gk, 0, 64))
            push(shard_ref, slot(gx, gk), 25, dev_s)
        elif stage == 1:
            push(shard_ref, slot(gx, gk), 6, dev_far)
        elif stage == 2:
            got(4, gx, ko, 0, 64, dev_o)
            forward(5, gx, ko, 0, 64, dev_i)
            line(h2_ids, ko, 32, 32)
            sibling(gx, ko, 0, 64)
            for side in range(2):
                x = sides[side][0]
                relay(0, side, gk, 0, 64)
                forward(h1_ids + 2 * side, x, gk, 0, 32, dev_o)
                sibling(x, gk, 0, 64)
        elif stage == 3:
            got(6, gx, kf, 0, 64, dev_far)
            line(h2_ids + 8, kf, 0, 64)
            sibling(gx, kf, 0, 64)
            far(0, gk, 0, 64)
            forward(h1_ids + 4, xo, gk, 0, 32, dev_o)
            sibling(xo, gk, 0, 64)
            for side in range(2):
                relay(h2_ids, side, ko, 32, 32)
            got(5, gx, ki, 0, 64, dev_i)
            line(h2_ids + 4, ki, 0, 64)
            sibling(gx, ki, 0, 64)
        elif stage == 4:
            for side in range(2):
                x = sides[side][0]
                got(h1_ids + 2 * side, x, ko, 0, 32, dev_o)
                sibling(x, ko, 0, 64)
            for side in range(2):
                relay(h2_ids + 8, side, kf, 0, 64)
                sibling(sides[side][0], kf, 0, 64)
        elif stage == 5:
            for side in range(2):
                relay(h2_ids + 4, side, ki, 0, 64)
                sibling(sides[side][0], ki, 0, 64)
            far(h2_ids, ko, 32, 32)
            got(h1_ids + 4, xo, ko, 0, 32, dev_o)
            sibling(xo, ko, 0, 64)
        else:
            far(h2_ids + 8, kf, 0, 64)
            sibling(xo, kf, 0, 64)
            far(h2_ids + 4, ki, 0, 64)
            sibling(xo, ki, 0, 64)

    gain = ngain_ref[...]
    load_x.wait()
    for at in range(0, TILE, 64):
        raw = xin[at // 4 : at // 4 + 16].astype(F32).reshape(64, WIDTH)
        xraw[at : at + 64] = raw.astype(BF16)
        mean = jnp.mean(raw, -1, keepdims=True)
        centered = raw - mean
        spread = jnp.mean(centered * centered, -1, keepdims=True)
        xn[at : at + 64] = (centered * lax.rsqrt(spread + 1e-05) * gain).astype(BF16)
    load_f.wait()
    for pair in range(2):
        fwd[pair] = dot(fwd_t[pair], xn[...]).astype(BF16)
        if pair == 0:
            pl.semaphore_wait(barrier, len(partners))
        for i, (at, rows) in enumerate(SENT):
            push(fwd.at[pair, pl.ds(at, rows)], rx.at[pair, pl.ds(at, rows)], 41 + 4 * pair + i, to[pair][i])

    gather(0)

    for pair in range(2):
        wrap = (lat == (nlat - 1 if pair == 0 else 0)).astype(jnp.int32)
        for w in range(2):
            codes = []
            for dim in range(2):
                at = lax.broadcasted_iota(jnp.int32, (WIN, WIN), dim)
                other = jnp.where(at < 72, 1, 0)
                level = ((at * 57) >> (11 - w)) & 1
                codes.append(other * wrap + 2 * level * pair)
            mask[pair, w] = jnp.where(codes[0] == codes[1], 1.0, 0.0)

    gather(1)
    load_q.wait()
    for pair in range(2):
        xquad[pair] = dot(quad_t[pair], xraw[...])

    gather(2)

    lane = lax.broadcasted_iota(jnp.int32, (1, 128), 1)
    low = jnp.where(lane < 64, 1.0, 0.0).astype(BF16)
    high = jnp.where(lane < 64, 0.0, 1.0).astype(BF16)

    def attend(pair, w, tokens):
        q = (dot(tokens, qkvw[:, :WIDTH]) * 0.125).astype(BF16)
        k = dot(tokens, qkvw[:, WIDTH : 2 * WIDTH]).astype(BF16)
        v = dot(tokens, qkvw[:, 2 * WIDTH :]).astype(BF16)
        same = mask[pair, w] > 0.5
        ones = jnp.ones((WIN, 128), BF16)
        for p in range(PAIRS):
            cols = slice(p * 128, (p + 1) * 128)
            both = jnp.concatenate([q[:, cols] * low, q[:, cols] * high], 0)
            scores = lax.dot_general(both, k[:, cols], (((1,), (1,)), ((), ())), preferred_element_type=F32)
            scores = jnp.where(same[None], scores.reshape(2, WIN, WIN), -1e30)
            top = jnp.max(scores, -1, keepdims=True)
            expo = jnp.exp(scores - top).astype(BF16).reshape(2 * WIN, WIN)
            result = dot(expo, jnp.concatenate([v[:, cols], ones], 1))
            result = result[:, :128] / result[:, 128:]
            att[pair, w, :, cols] = jnp.where(lane < 64, result[:WIN], result[WIN:]).astype(BF16)
        return dot(att[pair, w], projw[...]).astype(BF16)

    def send_back(pair, i):
        at, rows = SENT[i]
        push(bsend.at[pair, pl.ds(at, rows)], back.at[pair, pl.ds(at, rows)], 49 + 4 * pair + i, frm[pair][i])

    def await_piece(pair, i):
        at, rows = SENT[i]
        arrived(rx.at[pair, pl.ds(at, rows)], 41 + 4 * pair + i, frm[pair][i])

    load_qkv.wait()
    load_proj.wait()
    for pair in range(2):
        await_piece(pair, 0)
        s, own = rx.at[pair, pl.ds(0, 80)], fwd.at[pair, pl.ds(OWN, 80)]
        x = xw.at[pair, 0]
        x[0:64] = s[0:64]
        x[64:80] = s[64:80] + own[0:16]
        x[80:144] = own[16:80]
        branch = attend(pair, 0, x[...])
        bsend[pair, 0:80] = branch[0:80]
        send_back(pair, 0)
        back[pair, OWN : OWN + 80] = branch[64:144]

    for pair in range(2):
        for i in range(1, 4):
            await_piece(pair, i)
        s, l, d = (rx.at[pair, pl.ds(*SENT[i])] for i in range(1, 4))
        own = fwd.at[pair, pl.ds(OWN + 80, 48)]
        x = xw.at[pair, 1]
        x[0:32] = own[0:32]
        x[32:48] = own[32:48] + l[0:16]
        x[48:64] = l[16:32]
        x[64:80] = l[32:48] + s[0:16]
        x[80:96] = s[16:32]
        x[96:112] = s[32:48] + d[0:16]
        x[112:144] = d[16:48]
        branch = attend(pair, 1, x[...])
        bsend[pair, 80:128] = branch[64:112]
        bsend[pair, 128:176] = branch[32:80]
        bsend[pair, 176:224] = branch[96:144]
        for i in range(1, 4):
            send_back(pair, i)
        back[pair, OWN + 80 : PIECES] = branch[0:48]

    gather(3)
    gather(4)
    load_bq.wait()
    mgain = mgain_ref[...]
    for pair in range(2):
        for i, (at, rows) in enumerate(SENT):
            arrived(back.at[pair, pl.ds(at, rows)], 49 + 4 * pair + i, to[pair][i])
        if pair == 1:
            gather(5)
        quads = dot(backq_t[pair], back[pair]) + xquad[pair]
        quads = quads.astype(BF16).astype(F32).reshape(4, 72, WIDTH)
        mean = jnp.sum(jnp.sum(quads, 0), -1, keepdims=True) / (4 * WIDTH)
        centered = quads - mean
        spread = jnp.sum(jnp.sum(centered * centered, 0), -1, keepdims=True) / (4 * WIDTH)
        scale = lax.rsqrt(spread + 1e-05)
        for q in range(4):
            cols = slice(q * WIDTH, (q + 1) * WIDTH)
            mn[pair * 72 : (pair + 1) * 72, cols] = (centered[q] * scale * mgain[cols]).astype(BF16)

    load_b.wait()
    pieces = back[...].reshape(2 * PIECES, WIDTH)
    for at in range(0, TILE, 192):
        rows = dot(back_t[at : at + 192], pieces) + xraw[at : at + 192].astype(F32)
        out[at // 4 : at // 4 + 48] = rows.reshape(48, 4, WIDTH).astype(BF16)
    store_out = pltpu.make_async_copy(out, out_ref, local.at[9])
    store_out.start()

    gather(6)
    load_own.wait()
    load_order.wait()
    for ident, x, k, first, rows in siblings:
        arrived(slot(x, k, first, rows, 1 - core), ident, dev_s)

    def merge(n, carry):
        lanes = pl.ds(pl.multiple_of(n * 256, 256), 256)
        weight = wbuf[:, :, lanes].reshape(4 * WIDTH, 256)
        result = dot(mn[...], weight).astype(BF16)
        merged[:, :, lanes] = dot(order_t[...], result).reshape(36, 4, 256).astype(BF16)
        return carry

    lax.fori_loop(0, 4, merge, 0, unroll=True)
    store_merged = pltpu.make_async_copy(merged, coarse_ref, local.at[10])
    store_merged.start()

    for copy in started:
        copy.wait_send()
    store_out.wait()
    store_merged.wait()


def place(fine_ref, merged_ref, out_ref, coarse_ref, out, merged, came, left):
    parts = []
    for source, held, target in ((fine_ref, out, out_ref), (merged_ref, merged, coarse_ref)):
        rows = source.shape[0] // 4
        for i in range(4):
            at, part = pl.ds(i * rows, rows), len(parts)
            enter = pltpu.make_async_copy(source.at[at], held.at[at], came.at[part])
            enter.start()
            parts.append((enter, pltpu.make_async_copy(held.at[at], target.at[at], left.at[part])))
    for enter, leave in parts:
        enter.wait()
        leave.start()
    for _, leave in parts:
        leave.wait()


def local(fine_in, norm_gain, qkv_weight, proj_weight, merge_gain, merge_weight, *constants):
    anywhere = pl.BlockSpec(memory_space=pl.ANY)
    vmem = pl.BlockSpec(memory_space=pltpu.VMEM)
    scratch = [
        ((144, 4, WIDTH), BF16),
        ((TILE, WIDTH), BF16),
        ((TILE, WIDTH), BF16),
        ((2, PIECES, WIDTH), BF16),
        ((2, OWN, WIDTH), BF16),
        ((2, 2, WIN, WIDTH), BF16),
        ((2, 2, WIN, WIDTH), BF16),
        ((2, OWN, WIDTH), BF16),
        ((2, PIECES, WIDTH), BF16),
        ((2, 288, WIDTH), F32),
        ((2, 2, WIN, WIN), F32),
        ((144, 4 * WIDTH), BF16),
        ((36, 4, 2 * WIDTH), BF16),
        ((144, 4, WIDTH), BF16),
        ((32, 64, 2 * WIDTH), BF16),
        ((WIDTH, 3 * WIDTH), BF16),
        ((WIDTH, WIDTH), BF16),
        *((table.shape, BF16) for table in constants),
    ]
    tile = fine_in.transpose(1, 2, 0, 3).reshape(144, 4, WIDTH)
    out, coarse = pl.pallas_call(
        kernel,
        out_shape=(
            jax.ShapeDtypeStruct((144, 4, WIDTH), BF16),
            jax.ShapeDtypeStruct((36, 4, 2 * WIDTH), BF16),
        ),
        in_specs=[anywhere, vmem, anywhere, anywhere, vmem, anywhere] + [anywhere] * len(constants),
        out_specs=(anywhere, anywhere),
        scratch_shapes=[pltpu.VMEM(shape, dtype) for shape, dtype in scratch]
        + [pltpu.SemaphoreType.DMA((57,)), pltpu.SemaphoreType.DMA((57,)), pltpu.SemaphoreType.DMA((11,))],
        compiler_params=pltpu.CompilerParams(
            collective_id=0, has_side_effects=True, vmem_limit_bytes=56 * 1024 * 1024
        ),
        name="swin_block",
    )(tile, norm_gain, qkv_weight, proj_weight, merge_gain, merge_weight, *constants)
    fine_out, coarse = pl.pallas_call(
        place,
        out_shape=(jax.ShapeDtypeStruct(out.shape, BF16), jax.ShapeDtypeStruct(coarse.shape, BF16)),
        in_specs=[anywhere] * 2,
        out_specs=(anywhere, anywhere),
        scratch_shapes=[
            pltpu.VMEM(out.shape, BF16),
            pltpu.VMEM(coarse.shape, BF16),
            pltpu.SemaphoreType.DMA((8,)),
            pltpu.SemaphoreType.DMA((8,)),
        ],
        name="place",
    )(out, coarse)
    return (
        fine_out.reshape(12, 12, 4, WIDTH).transpose(2, 0, 1, 3),
        coarse.reshape(6, 6, 4, 2 * WIDTH).transpose(2, 0, 1, 3),
    )


def solution(mesh):
    grid = P(None, "lat", "lon", None)
    constants = tables()
    run = jax.shard_map(
        local,
        mesh=mesh,
        in_specs=(grid, P(), P(), P(), P(), P("lon", None), *(P() for _ in constants)),
        out_specs=(grid, grid),
        check_vma=False,
    )

    def whole(*arrays):
        return run(*arrays, *(jnp.asarray(table) for table in constants))

    return whole
```

```python
import functools

import jax
import jax.numpy as jnp
import numpy as np
from jax import lax
from jax.experimental import pallas as pl
from jax.experimental.pallas import tpu as pltpu
from jax.sharding import PartitionSpec as P

MESH = pl.DeviceIdType.MESH
BF16 = jnp.bfloat16
F32 = jnp.float32

WIDTH = 512
PAIRS = 4
WIN = 144
LEVELS = ((1, 2), (3, 0))
TILE = 576
SENT = ((0, 80), (80, 48), (128, 48), (176, 48))
OWN = 224
PIECES = 352


def tables():
    forward = np.zeros((2, PIECES, TILE), np.float32)
    quad = np.zeros((2, 288, TILE), np.float32)
    order = np.zeros((144, 144), np.float32)
    for pair in range(2):
        lo, hi = range(0, 6), range(6, 12)
        sent_rows, kept_rows = (lo, hi) if pair == 0 else (hi, lo)
        first, mid, last = range(0, 3), range(3, 9), range(9, 12)
        sent_cols, kept_cols = (first, last) if pair == 0 else (last, first)

        def put(at, rows, cols):
            for level in LEVELS[pair]:
                for r in rows:
                    for c in cols:
                        forward[pair, at, (r * 12 + c) * 4 + level] = 1
                        at += 1

        put(0, sent_rows, mid)
        put(80 + 8, sent_rows, kept_cols)
        put(128 + 4, kept_rows, sent_cols)
        put(176 + 12, sent_rows, sent_cols)
        put(OWN + 8, kept_rows, mid)
        put(OWN + 80, kept_rows, kept_cols)
        for l, level in enumerate(LEVELS[pair]):
            for r in range(12):
                for c in range(12):
                    q, at = (r % 2) + 2 * (c % 2), (r // 2) * 6 + c // 2
                    quad[pair, q * 72 + l * 36 + at, (r * 12 + c) * 4 + level] = 1
                    order[at * 4 + level, pair * 72 + l * 36 + at] = 1
    back = np.concatenate([forward[0].T, forward[1].T], 1)
    backq = np.stack([quad[pair] @ forward[pair].T for pair in range(2)])
    return [table.astype(BF16) for table in (forward, back, backq, quad, order)]


def dot(a, b):
    return jnp.dot(a, b, preferred_element_type=F32)


def kernel(
    fine_ref, ngain_ref, qkvw_ref, projw_ref, mgain_ref, shard_ref, fwd_ref, back_ref, backq_ref, quad_ref, order_ref,
    out_ref, coarse_ref,
    xin, xraw, xn, fwd, rx, xw, att, bsend, back, xquad, mask, mn, merged, out, wbuf,
    qkvw, projw, fwd_t, back_t, backq_t, quad_t, order_t, send, recv, local,
):
    ny = lax.axis_size("lat") // 2
    nlat, nlon = lax.axis_size("lat"), lax.axis_size("lon")
    lat, lon = lax.axis_index("lat"), lax.axis_index("lon")
    y, m = lat % ny, lat // ny
    gx, gk, core = lon // 8, (lon // 2) % 4, lon % 2
    up, down = (lat + nlat - 1) % nlat, (lat + 1) % nlat
    left, right = (lon + nlon - 1) % nlon, (lon + 1) % nlon

    xm, xp, xo = (gx + 3) % 4, (gx + 1) % 4, (gx + 2) % 4
    ko = (gk + 3 + 2 * m) % 4
    ki = (gk + 1 + 2 * m) % 4
    kf = (gk + 2) % 4
    olat = (1 - m) * ny + y
    dev_xp = (lat, xp * 8 + gk * 2 + core)
    dev_xm = (lat, xm * 8 + gk * 2 + core)
    dev_o = (olat, gx * 8 + ko * 2 + core)
    dev_i = (olat, lon)
    dev_far = (olat, gx * 8 + kf * 2 + core)
    dev_s = (lat, lon + 1 - 2 * core)
    to = (((up, lon), (up, lon), (lat, left), (up, left)), ((down, lon), (down, lon), (lat, right), (down, right)))
    frm = (to[1], to[0])

    barrier = pltpu.get_barrier_semaphore()
    partners = [*to[0][1:], *to[1][1:], dev_xp, dev_xm, dev_o, dev_i, dev_far, dev_s]
    for device in partners:
        pl.semaphore_signal(barrier, inc=1, device_id=device, device_id_type=MESH)

    copies = []

    def load(src, dst):
        copy = pltpu.make_async_copy(src, dst, local.at[len(copies)])
        copy.start()
        copies.append(copy)
        return copy

    load_x = load(fine_ref, xin)
    load_f = load(fwd_ref, fwd_t)
    load_qkv = load(qkvw_ref, qkvw)
    load_q = load(quad_ref, quad_t)
    load_proj = load(projw_ref, projw)
    load_bq = load(backq_ref, backq_t)
    load_b = load(back_ref, back_t)
    load_order = load(order_ref, order_t)
    load_own = load(shard_ref, wbuf.at[lon])

    started = []

    def push(src, dst, ident, device):
        copy = pltpu.make_async_remote_copy(
            src_ref=src, dst_ref=dst, send_sem=send.at[ident], recv_sem=recv.at[ident],
            device_id=device, device_id_type=MESH,
        )
        copy.start()
        started.append(copy)

    def arrived(dst, ident, device):
        pltpu.make_async_remote_copy(
            src_ref=dst, dst_ref=dst, send_sem=send.at[ident], recv_sem=recv.at[ident],
            device_id=device, device_id_type=MESH,
        ).wait_recv()

    def slot(x, k, first=0, rows=64, c=core):
        return wbuf.at[x * 8 + k * 2 + c, pl.ds(first, rows)]

    def forward(ident, x, k, first, rows, device):
        push(slot(x, k, first, rows), slot(x, k, first, rows), ident, device)

    def got(ident, x, k, first, rows, device):
        arrived(slot(x, k, first, rows), ident, device)

    siblings = []

    def sibling(x, k, first, rows):
        ident = 25 + len(siblings)
        siblings.append((ident, x, k, first, rows))
        forward(ident, x, k, first, rows, dev_s)

    h1_ids, h2_ids = 7, 13
    sides = ((xm, dev_xm, dev_xp), (xp, dev_xp, dev_xm))

    def line(ident, k, first, rows):
        forward(ident, gx, k, first, rows, dev_xp)
        forward(ident + 1, gx, k, first, rows, dev_xm)

    def relay(ident, side, k, first, rows):
        x, source, target = sides[side]
        got(ident + side, x, k, first, rows, source)
        forward(ident + 2 + side, x, k, first + side * rows // 2, rows // 2, target)

    def far(ident, k, first, rows):
        for side, (_, source, _) in enumerate(sides):
            got(ident + 2 + side, xo, k, first + side * rows // 2, rows // 2, source)

    def gather(stage):
        if stage == 0:
            for ident, device in ((4, dev_o), (0, dev_xp), (1, dev_xm)):
                push(shard_ref, slot(gx, gk), ident, device)
            siblings.append((25, gx, gk, 0, 64))
            push(shard_ref, slot(gx, gk), 25, dev_s)
        elif stage == 1:
            push(shard_ref, slot(gx, gk), 6, dev_far)
        elif stage == 2:
            got(4, gx, ko, 0, 64, dev_o)
            forward(5, gx, ko, 0, 64, dev_i)
            line(h2_ids, ko, 32, 32)
            sibling(gx, ko, 0, 64)
            for side in range(2):
                x = sides[side][0]
                relay(0, side, gk, 0, 64)
                forward(h1_ids + 2 * side, x, gk, 0, 32, dev_o)
                sibling(x, gk, 0, 64)
        elif stage == 3:
            got(6, gx, kf, 0, 64, dev_far)
            line(h2_ids + 8, kf, 0, 64)
            sibling(gx, kf, 0, 64)
            far(0, gk, 0, 64)
            forward(h1_ids + 4, xo, gk, 0, 32, dev_o)
            sibling(xo, gk, 0, 64)
            for side in range(2):
                relay(h2_ids, side, ko, 32, 32)
            got(5, gx, ki, 0, 64, dev_i)
            line(h2_ids + 4, ki, 0, 64)
            sibling(gx, ki, 0, 64)
        elif stage == 4:
            for side in range(2):
                x = sides[side][0]
                got(h1_ids + 2 * side, x, ko, 0, 32, dev_o)
                sibling(x, ko, 0, 64)
            for side in range(2):
                relay(h2_ids + 8, side, kf, 0, 64)
                sibling(sides[side][0], kf, 0, 64)
        elif stage == 5:
            for side in range(2):
                relay(h2_ids + 4, side, ki, 0, 64)
                sibling(sides[side][0], ki, 0, 64)
            far(h2_ids, ko, 32, 32)
            got(h1_ids + 4, xo, ko, 0, 32, dev_o)
            sibling(xo, ko, 0, 64)
        else:
            far(h2_ids + 8, kf, 0, 64)
            sibling(xo, kf, 0, 64)
            far(h2_ids + 4, ki, 0, 64)
            sibling(xo, ki, 0, 64)

    gain = ngain_ref[...]
    load_x.wait()
    for at in range(0, TILE, 64):
        raw = xin[at // 4 : at // 4 + 16].astype(F32).reshape(64, WIDTH)
        xraw[at : at + 64] = raw.astype(BF16)
        mean = jnp.mean(raw, -1, keepdims=True)
        centered = raw - mean
        spread = jnp.mean(centered * centered, -1, keepdims=True)
        xn[at : at + 64] = (centered * lax.rsqrt(spread + 1e-05) * gain).astype(BF16)
    load_f.wait()
    for pair in range(2):
        fwd[pair] = dot(fwd_t[pair], xn[...]).astype(BF16)
        if pair == 0:
            pl.semaphore_wait(barrier, len(partners))
        for i, (at, rows) in enumerate(SENT):
            push(fwd.at[pair, pl.ds(at, rows)], rx.at[pair, pl.ds(at, rows)], 41 + 4 * pair + i, to[pair][i])

    gather(0)

    for pair in range(2):
        wrap = (lat == (nlat - 1 if pair == 0 else 0)).astype(jnp.int32)
        for w in range(2):
            codes = []
            for dim in range(2):
                at = lax.broadcasted_iota(jnp.int32, (WIN, WIN), dim)
                other = jnp.where(at < 72, 1, 0)
                level = ((at * 57) >> (11 - w)) & 1
                codes.append(other * wrap + 2 * level * pair)
            mask[pair, w] = jnp.where(codes[0] == codes[1], 1.0, 0.0)

    gather(1)
    load_q.wait()
    for pair in range(2):
        xquad[pair] = dot(quad_t[pair], xraw[...])

    gather(2)

    lane = lax.broadcasted_iota(jnp.int32, (1, 128), 1)
    low = jnp.where(lane < 64, 1.0, 0.0).astype(BF16)
    high = jnp.where(lane < 64, 0.0, 1.0).astype(BF16)

    def attend(pair, w, tokens):
        q = (dot(tokens, qkvw[:, :WIDTH]) * 0.125).astype(BF16)
        k = dot(tokens, qkvw[:, WIDTH : 2 * WIDTH]).astype(BF16)
        v = dot(tokens, qkvw[:, 2 * WIDTH :]).astype(BF16)
        same = mask[pair, w] > 0.5
        ones = jnp.ones((WIN, 128), BF16)
        for p in range(PAIRS):
            cols = slice(p * 128, (p + 1) * 128)
            both = jnp.concatenate([q[:, cols] * low, q[:, cols] * high], 0)
            scores = lax.dot_general(both, k[:, cols], (((1,), (1,)), ((), ())), preferred_element_type=F32)
            scores = jnp.where(same[None], scores.reshape(2, WIN, WIN), -1e30)
            top = jnp.max(scores, -1, keepdims=True)
            expo = jnp.exp(scores - top).astype(BF16).reshape(2 * WIN, WIN)
            result = dot(expo, jnp.concatenate([v[:, cols], ones], 1))
            result = result[:, :128] / result[:, 128:]
            att[pair, w, :, cols] = jnp.where(lane < 64, result[:WIN], result[WIN:]).astype(BF16)
        return dot(att[pair, w], projw[...]).astype(BF16)

    def send_back(pair, i):
        at, rows = SENT[i]
        push(bsend.at[pair, pl.ds(at, rows)], back.at[pair, pl.ds(at, rows)], 49 + 4 * pair + i, frm[pair][i])

    def await_piece(pair, i):
        at, rows = SENT[i]
        arrived(rx.at[pair, pl.ds(at, rows)], 41 + 4 * pair + i, frm[pair][i])

    load_qkv.wait()
    load_proj.wait()
    for pair in range(2):
        await_piece(pair, 0)
        s, own = rx.at[pair, pl.ds(0, 80)], fwd.at[pair, pl.ds(OWN, 80)]
        x = xw.at[pair, 0]
        x[0:64] = s[0:64]
        x[64:80] = s[64:80] + own[0:16]
        x[80:144] = own[16:80]
        branch = attend(pair, 0, x[...])
        bsend[pair, 0:80] = branch[0:80]
        send_back(pair, 0)
        back[pair, OWN : OWN + 80] = branch[64:144]

    for pair in range(2):
        for i in range(1, 4):
            await_piece(pair, i)
        s, l, d = (rx.at[pair, pl.ds(*SENT[i])] for i in range(1, 4))
        own = fwd.at[pair, pl.ds(OWN + 80, 48)]
        x = xw.at[pair, 1]
        x[0:32] = own[0:32]
        x[32:48] = own[32:48] + l[0:16]
        x[48:64] = l[16:32]
        x[64:80] = l[32:48] + s[0:16]
        x[80:96] = s[16:32]
        x[96:112] = s[32:48] + d[0:16]
        x[112:144] = d[16:48]
        branch = attend(pair, 1, x[...])
        bsend[pair, 80:128] = branch[64:112]
        bsend[pair, 128:176] = branch[32:80]
        bsend[pair, 176:224] = branch[96:144]
        for i in range(1, 4):
            send_back(pair, i)
        back[pair, OWN + 80 : PIECES] = branch[0:48]

    gather(3)
    gather(4)
    load_bq.wait()
    mgain = mgain_ref[...]
    for pair in range(2):
        for i, (at, rows) in enumerate(SENT):
            arrived(back.at[pair, pl.ds(at, rows)], 49 + 4 * pair + i, to[pair][i])
        if pair == 1:
            gather(5)
        quads = dot(backq_t[pair], back[pair]) + xquad[pair]
        quads = quads.astype(BF16).astype(F32).reshape(4, 72, WIDTH)
        mean = jnp.sum(jnp.sum(quads, 0), -1, keepdims=True) / (4 * WIDTH)
        centered = quads - mean
        spread = jnp.sum(jnp.sum(centered * centered, 0), -1, keepdims=True) / (4 * WIDTH)
        scale = lax.rsqrt(spread + 1e-05)
        for q in range(4):
            cols = slice(q * WIDTH, (q + 1) * WIDTH)
            mn[pair * 72 : (pair + 1) * 72, cols] = (centered[q] * scale * mgain[cols]).astype(BF16)

    load_b.wait()
    pieces = back[...].reshape(2 * PIECES, WIDTH)
    for at in range(0, TILE, 192):
        rows = dot(back_t[at : at + 192], pieces) + xraw[at : at + 192].astype(F32)
        out[at // 4 : at // 4 + 48] = rows.reshape(48, 4, WIDTH).astype(BF16)
    store_out = pltpu.make_async_copy(out, out_ref, local.at[9])
    store_out.start()

    gather(6)
    load_own.wait()
    load_order.wait()
    for ident, x, k, first, rows in siblings:
        arrived(slot(x, k, first, rows, 1 - core), ident, dev_s)

    stores = [store_out]
    for n in range(4):
        lanes = pl.ds(n * 256, 256)
        weight = wbuf[:, :, lanes].reshape(4 * WIDTH, 256)
        result = dot(mn[...], weight).astype(BF16)
        merged[:, :, lanes] = dot(order_t[...], result).reshape(36, 4, 256).astype(BF16)
        store = pltpu.make_async_copy(merged.at[:, :, lanes], coarse_ref.at[:, :, lanes], local.at[10 + n])
        store.start()
        stores.append(store)

    for copy in started:
        copy.wait_send()
    for store in stores:
        store.wait()


def place(fine_ref, merged_ref, out_ref, coarse_ref, out, merged, came, left):
    parts = []
    for source, held, target in ((fine_ref, out, out_ref), (merged_ref, merged, coarse_ref)):
        rows = source.shape[0] // 4
        for i in range(4):
            at, part = pl.ds(i * rows, rows), len(parts)
            enter = pltpu.make_async_copy(source.at[at], held.at[at], came.at[part])
            enter.start()
            parts.append((enter, pltpu.make_async_copy(held.at[at], target.at[at], left.at[part])))
    for enter, leave in parts:
        enter.wait()
        leave.start()
    for _, leave in parts:
        leave.wait()


def local(fine_in, norm_gain, qkv_weight, proj_weight, merge_gain, merge_weight, *constants):
    anywhere = pl.BlockSpec(memory_space=pl.ANY)
    vmem = pl.BlockSpec(memory_space=pltpu.VMEM)
    scratch = [
        ((144, 4, WIDTH), BF16),
        ((TILE, WIDTH), BF16),
        ((TILE, WIDTH), BF16),
        ((2, PIECES, WIDTH), BF16),
        ((2, OWN, WIDTH), BF16),
        ((2, 2, WIN, WIDTH), BF16),
        ((2, 2, WIN, WIDTH), BF16),
        ((2, OWN, WIDTH), BF16),
        ((2, PIECES, WIDTH), BF16),
        ((2, 288, WIDTH), F32),
        ((2, 2, WIN, WIN), F32),
        ((144, 4 * WIDTH), BF16),
        ((36, 4, 2 * WIDTH), BF16),
        ((144, 4, WIDTH), BF16),
        ((32, 64, 2 * WIDTH), BF16),
        ((WIDTH, 3 * WIDTH), BF16),
        ((WIDTH, WIDTH), BF16),
        *((table.shape, BF16) for table in constants),
    ]
    tile = fine_in.transpose(1, 2, 0, 3).reshape(144, 4, WIDTH)
    out, coarse = pl.pallas_call(
        kernel,
        out_shape=(
            jax.ShapeDtypeStruct((144, 4, WIDTH), BF16),
            jax.ShapeDtypeStruct((36, 4, 2 * WIDTH), BF16),
        ),
        in_specs=[anywhere, vmem, anywhere, anywhere, vmem, anywhere] + [anywhere] * len(constants),
        out_specs=(anywhere, anywhere),
        scratch_shapes=[pltpu.VMEM(shape, dtype) for shape, dtype in scratch]
        + [pltpu.SemaphoreType.DMA((57,)), pltpu.SemaphoreType.DMA((57,)), pltpu.SemaphoreType.DMA((14,))],
        compiler_params=pltpu.CompilerParams(
            collective_id=0, has_side_effects=True, vmem_limit_bytes=56 * 1024 * 1024
        ),
        name="swin_block",
    )(tile, norm_gain, qkv_weight, proj_weight, merge_gain, merge_weight, *constants)
    fine_out, coarse = pl.pallas_call(
        place,
        out_shape=(jax.ShapeDtypeStruct(out.shape, BF16), jax.ShapeDtypeStruct(coarse.shape, BF16)),
        in_specs=[anywhere] * 2,
        out_specs=(anywhere, anywhere),
        scratch_shapes=[
            pltpu.VMEM(out.shape, BF16),
            pltpu.VMEM(coarse.shape, BF16),
            pltpu.SemaphoreType.DMA((8,)),
            pltpu.SemaphoreType.DMA((8,)),
        ],
        name="place",
    )(out, coarse)
    return (
        fine_out.reshape(12, 12, 4, WIDTH).transpose(2, 0, 1, 3),
        coarse.reshape(6, 6, 4, 2 * WIDTH).transpose(2, 0, 1, 3),
    )


def solution(mesh):
    grid = P(None, "lat", "lon", None)
    constants = tables()
    run = jax.shard_map(
        local,
        mesh=mesh,
        in_specs=(grid, P(), P(), P(), P(), P("lon", None), *(P() for _ in constants)),
        out_specs=(grid, grid),
        check_vma=False,
    )

    def whole(*arrays):
        return run(*arrays, *(jnp.asarray(table) for table in constants))

    return whole
```
